32 devices in a mesh: section: 2 (over core), expert: 4 (over y, x), replica: 4 (over z).
Axes of the slice: x: 2, y: 2, z: 4, core: 2. Of those that a mesh axis runs over, the one named last changes fastest.
Arguments:
- forward_tokens: bfloat16 [2, 2048, 2048], P('section', ('expert', 'replica')), may hold values from -6 to 6
- forward_routes: int32 [2, 2048, 1], P('section', ('expert', 'replica')), may hold values from 0 to 3; in each aligned block of 128 rows (0 to 127, 128 to 255, ..., all dimensions but the last counted through in order) at most 48 rows name the same one
- forward_gates: float32 [2, 2048, 1], P('section', ('expert', 'replica')), may hold values from 0.1 to 1
- backward_cotangent: bfloat16 [2, 2048, 2048], P('section', ('expert', 'replica')), may hold values from -6 to 6
- backward_routes: int32 [2, 2048, 1], P('section', ('expert', 'replica')), may hold values from 0 to 3; in each aligned block of 128 rows (0 to 127, 128 to 255, ..., all dimensions but the last counted through in order) at most 48 rows name the same one
- backward_gates: float32 [2, 2048, 1], P('section', ('expert', 'replica')), may hold values from 0.1 to 1
- saved_rows: bfloat16 [2, 4, 768, 2048], P('section', 'expert', 'replica'), may hold values from -6 to 6
- gate_weight: bfloat16 [2, 4, 2048, 384], P('section', 'expert'), may hold values from -0.125 to 0.125
- up_weight: bfloat16 [2, 4, 2048, 384], P('section', 'expert'), may hold values from -0.125 to 0.125
- down_weight: bfloat16 [2, 4, 2048, 384], P('section', 'expert'), may hold values from -0.3125 to 0.3125
Outputs:
- forward_out: bfloat16 [2, 2048, 2048], P('section', ('expert', 'replica'))
- received_grad: bfloat16 [2, 2048, 2048], P('section', ('expert', 'replica'))
- expert_grads: bfloat16 [2, 4, 2048, 768], P('section', 'expert', 'replica')
The draws below stay inside these ranges and needn't reach their ends.
Inputs may be any that keep to these rules, and one draw needn't show every extreme that they name: `forward_routes`: each is an expert in flight. Among the rows of one device, no expert is named more than 48 times, and some expert reaches 48. `backward_routes`: each is an expert in flight. Among the rows of one device, no expert is named more than 48 times, and some expert reaches 48.
All inputs are finite; a program needn't handle non-finite values.
Results may differ from the reference program's by a relative error of at most 0.017.
Values may be sent and summed in bfloat16 or wider, within the bound.
A program may use at most 64 MiB of HBM per device.

```python
import math
import jax
import jax.numpy as jnp
import numpy as np
from jax import lax

D = 2048
FF = 384
TOK_DEV = 128
TOP = 1
SECTIONS = 2
EXPERTS = 4
REPS = 4
CAP = 48
TOKENS = 2048


def raised(values, stream_key, source, target, parts, factor):
    def block_of(position):
        return (jnp.arange(values.shape[position]) // (values.shape[position] // parts)).reshape((-1,) + (1,) * (values.ndim - 1 - position))

    one_side = jax.random.permutation(stream_key, parts)[block_of(target)]
    second = (block_of(target) + parts // 2) % parts
    return jnp.where((block_of(source) == one_side) | (block_of(source) == second), factor * values, values)


def block_levels(key, dims, shards, least, high):
    factor_of, own = 1.0, jax.random.fold_in(key, 6)
    for axis_at, parts in shards:
        heights = jnp.exp(jax.random.uniform(jax.random.fold_in(own, axis_at), (parts,), jnp.float32, least / len(shards), high / len(shards)))
        factor_of = factor_of * jnp.repeat(heights, dims[axis_at] // parts).reshape([-1 if axis == axis_at else 1 for axis in range(len(dims))])
    return factor_of


def deal_out(key, own, number, rows, amount, top, reach, slope):
    order = jax.random.permutation(key, amount)
    packed, ordinary = load_shares(amount, rows * top, reach, slope, True), load_shares(amount, rows * top, reach, slope, False)
    places = jnp.arange(amount)

    def named(tallies, turn):
        used = int((tallies > 0).sum())
        fixed = max(1, used // 4)
        shifted = fixed + (places - fixed + turn * (used - fixed)) % max(1, amount - fixed)
        return jnp.zeros((amount,), jnp.int32).at[order[jnp.where(places < fixed, places, shifted)]].set(jnp.asarray(tallies, jnp.int32))

    tallies = jnp.where(number % 4 == 0, named(packed, number // 4), named(ordinary, number - number // 4 - 1))
    mixed = jax.random.permutation(jax.random.fold_in(own, 3), amount)
    giver, sink = mixed[0:amount // 2 * 2:2], mixed[1:amount // 2 * 2:2]
    margin = jnp.minimum(tallies[giver] - 1, reach - tallies[sink]) // 2
    margin = jnp.where((giver == order[0]) | (sink == order[0]) | (tallies[sink] == 0), 0, jnp.maximum(margin, 0))
    shifted = jax.random.randint(jax.random.fold_in(own, 4), (amount // 2,), 0, 1 << 20) % (margin + 1)
    tallies = tallies.at[giver].add(-shifted).at[sink].add(shifted)
    members = jnp.searchsorted(jnp.cumsum(tallies), jnp.arange(rows * top), side="right").astype(jnp.int32)
    grid = members.reshape(top, rows).T
    grid = grid[jax.random.permutation(jax.random.fold_in(own, 1), rows)]
    turn = jax.random.randint(jax.random.fold_in(own, 2), (rows, 1), 0, top)
    return jnp.take_along_axis(grid, (jnp.arange(top)[None, :] + turn) % top, axis=1)


def load_shares(number_of, total, reach, skew, full):
    loads = [(1 << 20) // math.isqrt(standing ** skew) + 1 for standing in range(1, number_of + 1)]
    largest = reach if full else min(reach, max(-(-total // number_of), total * loads[0] // sum(loads)))
    least = 1 if total - largest >= number_of - 1 else 0
    given, spare = [largest] + [least] * (number_of - 1), total - largest - least * (number_of - 1)
    while spare > 0:
        candidates = [i for i in range(1, number_of) if given[i] < largest] or [i for i in range(1, number_of) if given[i] < reach]
        pool, remaining = sum([loads[i] for i in candidates]), spare
        for i in candidates:
            more = min(reach - given[i], max(1, remaining * loads[i] // pool), spare)
            given[i] = given[i] + more
            spare = spare - more
    return np.array(given)


def centred(own_key, dims, scale, bound, split=(), held_as=jnp.bfloat16):
    values = scale * jax.random.normal(own_key, dims, jnp.float32)
    if split:
        values = values * block_levels(own_key, dims, split, -0.22, 0.18)
    return jnp.clip(values, -bound, bound).astype(held_as)


def bell_draw_with(own_key, extent, scale, most, pieces, heavy, kind=jnp.bfloat16):
    drawn = scale * jax.random.normal(own_key, extent, jnp.float32)
    if pieces:
        drawn = drawn * block_levels(own_key, extent, pieces, -0.22, 0.18)
    return jnp.clip(raised(drawn, jax.random.fold_in(own_key, 3), *heavy), -most, most).astype(kind)


def setup_inputs(seed: int = 0) -> dict:
    splits = jax.random.split(jax.random.key(seed), 11)
    forward_tokens = centred(splits[0], (SECTIONS, TOKENS, D), 1.0, 6.0, ((0, 2), (1, 16)))
    forward_routes_keys = jax.random.split(jax.random.fold_in(splits[1], 1), SECTIONS * TOKENS // TOK_DEV)
    forward_routes_turns = jax.random.permutation(jax.random.fold_in(splits[1], 3), SECTIONS * TOKENS // TOK_DEV)
    forward_routes = jax.vmap(lambda own, number: deal_out(jax.random.fold_in(splits[1], 2), own, number, TOK_DEV, EXPERTS, TOP, CAP, 2))(forward_routes_keys, forward_routes_turns).reshape((SECTIONS, TOKENS, TOP))
    forward_gates = jnp.clip(0.1 + 0.9 * jax.random.uniform(splits[2], (SECTIONS, TOKENS, TOP), jnp.float32) ** block_levels(splits[2], (SECTIONS, TOKENS, TOP), ((0, 2), (1, 16)), -0.2, 0.2), 0.1, 1.0)
    backward_cotangent = centred(splits[3], (SECTIONS, TOKENS, D), 1.0, 6.0, ((0, 2), (1, 16)))
    backward_routes_keys = jax.random.split(jax.random.fold_in(splits[4], 1), SECTIONS * TOKENS // TOK_DEV)
    backward_routes_turns = jax.random.permutation(jax.random.fold_in(splits[4], 3), SECTIONS * TOKENS // TOK_DEV)
    backward_routes = jax.vmap(lambda own, number: deal_out(jax.random.fold_in(splits[4], 2), own, number, TOK_DEV, EXPERTS, TOP, CAP, 2))(backward_routes_keys, backward_routes_turns).reshape((SECTIONS, TOKENS, TOP))
    backward_gates = jnp.clip(0.1 + 0.9 * jax.random.uniform(splits[5], (SECTIONS, TOKENS, TOP), jnp.float32) ** block_levels(splits[5], (SECTIONS, TOKENS, TOP), ((0, 2), (1, 16)), -0.2, 0.2), 0.1, 1.0)
    saved_rows = bell_draw_with(splits[6], (SECTIONS, EXPERTS, REPS * EXPERTS * CAP, D), 1.0, 6.0, ((0, 2), (1, 4), (2, 4)), (2, 3, 4, 2.0))
    gate_weight = centred(splits[7], (SECTIONS, EXPERTS, D, FF), D ** -0.5, 0.125, ((0, 2), (1, 4)))
    up_weight = centred(splits[8], (SECTIONS, EXPERTS, D, FF), D ** -0.5, 0.125, ((0, 2), (1, 4)))
    down_weight = centred(splits[9], (SECTIONS, EXPERTS, D, FF), FF ** -0.5, 0.3125, ((0, 2), (1, 4)))
    return {"forward_tokens": forward_tokens, "forward_routes": forward_routes, "forward_gates": forward_gates, "backward_cotangent": backward_cotangent, "backward_routes": backward_routes, "backward_gates": backward_gates, "saved_rows": saved_rows, "gate_weight": gate_weight, "up_weight": up_weight, "down_weight": down_weight}


def slot_tables(routes):
    blocks = routes.reshape(TOKENS // TOK_DEV, TOK_DEV * TOP)
    member = (blocks[:, :, None] == jnp.arange(EXPERTS, dtype=jnp.int32)[None, None, :]).astype(jnp.int32)
    earlier = jnp.cumsum(member, axis=1) - member
    slot_index = jnp.sum(earlier * member, axis=2).astype(jnp.int32)
    return blocks, slot_index


def dispatch(values, blocks, slot_index):
    block_count = TOKENS // TOK_DEV
    block_index = jnp.broadcast_to(jnp.arange(block_count, dtype=jnp.int32)[:, None], blocks.shape)
    buffer = jnp.zeros((block_count, EXPERTS, CAP, D), values.dtype)
    buffer = buffer.at[block_index, blocks, slot_index].add(values)
    buffer = buffer.reshape(EXPERTS, REPS, EXPERTS, CAP, D).transpose(2, 1, 0, 3, 4)
    return buffer.reshape(EXPERTS, REPS * EXPERTS * CAP, D)


def collect(row_block, blocks, slot_index):
    block_count = TOKENS // TOK_DEV
    buffer = row_block.reshape(EXPERTS, REPS, EXPERTS, CAP, D).transpose(2, 1, 0, 3, 4)
    buffer = buffer.reshape(block_count, EXPERTS, CAP, D)
    block_index = jnp.broadcast_to(jnp.arange(block_count, dtype=jnp.int32)[:, None], blocks.shape)
    return buffer[block_index, blocks, slot_index]


def expert_forward(operands):
    row_block, w_gate, w_up, w_down = operands
    gate_pre = jnp.dot(row_block, w_gate, preferred_element_type=jnp.float32)
    up_pre = jnp.dot(row_block, w_up, preferred_element_type=jnp.float32)
    hidden = (gate_pre * jax.nn.sigmoid(gate_pre) * up_pre).astype(jnp.bfloat16)
    result = lax.dot_general(hidden, w_down, (((1,), (1,)), ((), ())), preferred_element_type=jnp.float32)
    return result.astype(jnp.bfloat16)


def expert_backward(operands):
    row_block, cot_block, w_gate, w_up, w_down = operands
    gate_pre = jnp.dot(row_block, w_gate, preferred_element_type=jnp.float32)
    up_pre = jnp.dot(row_block, w_up, preferred_element_type=jnp.float32)
    sigma = jax.nn.sigmoid(gate_pre)
    hidden_grad = jnp.dot(cot_block, w_down, preferred_element_type=jnp.float32)
    up_grad = (hidden_grad * gate_pre * sigma).astype(jnp.bfloat16)
    gate_grad = (hidden_grad * up_pre * sigma * (1.0 + gate_pre * (1.0 - sigma))).astype(jnp.bfloat16)
    contract = (((1,), (1,)), ((), ()))
    row_grad = lax.dot_general(gate_grad, w_gate, contract, preferred_element_type=jnp.float32)
    row_grad = row_grad + lax.dot_general(up_grad, w_up, contract, preferred_element_type=jnp.float32)
    return row_grad.astype(jnp.bfloat16), gate_grad, up_grad


def replica_sums(row_block, gate_grad, up_grad):
    def partial_term(operands):
        part_rows, part_grads = operands
        contract = (((0,), (0,)), ((), ()))
        term = lax.dot_general(part_rows, part_grads, contract, preferred_element_type=jnp.float32)
        return term.astype(jnp.bfloat16)

    both = jnp.concatenate([gate_grad, up_grad], axis=1)
    rows_split = row_block.reshape(REPS, EXPERTS * CAP, D)
    grads_split = both.reshape(REPS, EXPERTS * CAP, 2 * FF)
    partials = lax.map(partial_term, (rows_split, grads_split))
    return jnp.sum(partials.astype(jnp.float32), axis=0).astype(jnp.bfloat16)


def section_pass(operands):
    (forward_tokens, forward_routes, forward_gates, backward_cotangent, backward_routes, backward_gates, saved_rows, gate_weight, up_weight, down_weight) = operands
    block_count = TOKENS // TOK_DEV
    blocks, slot_index = slot_tables(forward_routes)
    grouped = forward_tokens.reshape(block_count, TOK_DEV, 1, D)
    copies = jnp.broadcast_to(grouped, (block_count, TOK_DEV, TOP, D)).reshape(block_count, TOK_DEV * TOP, D)
    expert_rows = dispatch(copies, blocks, slot_index)
    outputs = lax.map(expert_forward, (expert_rows, gate_weight, up_weight, down_weight))
    returned = collect(outputs, blocks, slot_index).astype(jnp.float32)
    weighted = returned * forward_gates.reshape(block_count, TOK_DEV * TOP, 1)
    mixed = jnp.sum(weighted.reshape(TOKENS, TOP, D), axis=1)
    forward_out = (forward_tokens.astype(jnp.float32) + mixed).astype(jnp.bfloat16)

    back_blocks, back_slots = slot_tables(backward_routes)
    scaled = backward_gates.reshape(TOKENS, TOP, 1) * backward_cotangent.astype(jnp.float32)[:, None, :]
    scaled = scaled.astype(jnp.bfloat16).reshape(block_count, TOK_DEV * TOP, D)
    cot_rows = dispatch(scaled, back_blocks, back_slots)

    def per_expert(inner):
        row_block, cot_block, w_gate, w_up, w_down = inner
        row_grad, gate_grad, up_grad = expert_backward((row_block, cot_block, w_gate, w_up, w_down))
        return row_grad, replica_sums(row_block, gate_grad, up_grad)

    row_grads, weight_grads = lax.map(per_expert, (saved_rows, cot_rows, gate_weight, up_weight, down_weight))
    back = collect(row_grads, back_blocks, back_slots).astype(jnp.float32).reshape(TOKENS, TOP, D)
    local_grad = (backward_cotangent.astype(jnp.float32) + jnp.sum(back, axis=1)).astype(jnp.bfloat16)
    return forward_out, local_grad, weight_grads


def reference(forward_tokens, forward_routes, forward_gates, backward_cotangent, backward_routes, backward_gates, saved_rows, gate_weight, up_weight, down_weight):
    forward_out, local_grad, weight_grads = lax.map(section_pass, (forward_tokens, forward_routes, forward_gates, backward_cotangent, backward_routes, backward_gates, saved_rows, gate_weight, up_weight, down_weight))
    received_grad = jnp.roll(local_grad, -1, axis=0)
    return forward_out, received_grad, weight_grads
```

```python
import functools

import jax
import jax.numpy as jnp
from jax import lax
from jax.experimental import pallas as pl
from jax.experimental.pallas import tpu as pltpu
from jax.sharding import PartitionSpec as P

MESH = pl.DeviceIdType.MESH
BF16, F32 = jnp.bfloat16, jnp.float32


def flipped(index, mask):
    for bit in range(mask.bit_length()):
        if (mask >> bit) & 1:
            index = index + (1 << bit) * (1 - 2 * ((index // (1 << bit)) % 2))
    return index


def route_slots(routes, experts, cap):
    tokens = routes.shape[1]
    height = -(-experts // 16) * 16
    member = (lax.broadcasted_iota(jnp.int32, (height, tokens), 0) == routes).astype(F32)
    above = lax.broadcasted_iota(jnp.int32, (tokens, tokens), 0)
    across = lax.broadcasted_iota(jnp.int32, (tokens, tokens), 1)
    before = (above < across).astype(F32).astype(BF16)
    earlier = jnp.dot(member.astype(BF16), before, preferred_element_type=F32)
    slot = jnp.sum(earlier * member, axis=0, keepdims=True)
    row = routes.astype(F32) * cap + slot
    return row, to_column(row)


def to_column(row):
    tokens = row.shape[1]
    above = lax.broadcasted_iota(jnp.int32, (tokens, tokens), 0)
    across = lax.broadcasted_iota(jnp.int32, (tokens, tokens), 1)
    return jnp.sum(jnp.where(above == across, row, 0.0), axis=1, keepdims=True)


def spread_table(column, rows):
    across = lax.broadcasted_iota(jnp.int32, (column.shape[0], rows), 1).astype(F32)
    return (across == column).astype(F32).astype(BF16)


def transposed_dot(a, b):
    return lax.dot_general(a, b, (((1,), (1,)), ((), ())), preferred_element_type=F32)


def kernel(
    sections, experts, replicas, cap,
    f_routes, f_gates, b_routes, b_gates, tokens_hbm, cot_hbm, saved_hbm, gate_hbm, up_hbm, down_hbm,
    out_hbm, received_hbm, grads_hbm,
    tokens, cot, saved, w_gu, w_down, f_send, f_recv, b_send, b_recv,
    o_send, o_recv, r_send, r_recv, x_all, g_all, pre, out_v, local_v, grads_v,
    local_sem, a2a_send, a2a_recv, x_send, x_recv, g_send, g_recv, s_send, s_recv, out_sem,
):
    section, me, rep = lax.axis_index("section"), lax.axis_index("expert"), lax.axis_index("replica")
    count, width = tokens.shape
    rows = experts * cap
    hidden_units = w_down.shape[1]
    share = width // replicas
    chunk = min(512, width)

    barrier = pltpu.get_barrier_semaphore()
    greeted = 0
    for k in range(1, experts):
        pl.semaphore_signal(barrier, inc=1, device_id={"expert": flipped(me, k)}, device_id_type=MESH)
        greeted += 1
    for k in range(1, replicas):
        pl.semaphore_signal(barrier, inc=1, device_id={"replica": (rep + k) % replicas}, device_id_type=MESH)
        greeted += 1
    for k in sorted({1, sections - 1}):
        pl.semaphore_signal(barrier, inc=1, device_id={"section": (section + k) % sections}, device_id_type=MESH)
        greeted += 1

    loads = [
        pltpu.make_async_copy(src, dst, local_sem.at[i])
        for i, (src, dst) in enumerate([
            (cot_hbm, cot),
            (tokens_hbm, tokens),
            (saved_hbm, saved),
            (gate_hbm, w_gu.at[:, pl.ds(0, hidden_units)]),
            (up_hbm, w_gu.at[:, pl.ds(hidden_units, hidden_units)]),
            (down_hbm, w_down),
            (saved_hbm.at[:, pl.ds(pl.multiple_of(rep * share, share), share)],
             x_all.at[pl.ds(pl.multiple_of(rep * rows, rows), rows)]),
        ])
    ]
    for load in loads:
        load.start()

    def block(ref, index):
        return ref.at[pl.ds(pl.multiple_of(index * cap, cap), cap)]

    def exchange(phase, k, src, dst):
        other = flipped(me, k)
        return pltpu.make_async_remote_copy(
            src_ref=block(src, other), dst_ref=block(dst, me),
            send_sem=a2a_send.at[phase, k], recv_sem=a2a_recv.at[phase, k],
            device_id={"expert": other}, device_id_type=MESH,
        )

    order = list(range(experts - 1, 0, -1))

    def pack(row, values, index):
        down = lax.broadcasted_iota(jnp.int32, (cap, count), 0).astype(F32) + (index * cap).astype(F32)
        table = (down == row).astype(F32).astype(BF16)
        return jnp.dot(table, values, preferred_element_type=F32).astype(BF16)

    b_row, b_column = route_slots(b_routes[...], experts, cap)
    b_scale = to_column(b_gates[...])
    loads[0].wait()
    scaled = (b_scale * cot[...].astype(F32)).astype(BF16)
    phases = [[], [], [], []]
    for k in order:
        block(b_send, flipped(me, k))[...] = pack(b_row, scaled, flipped(me, k))
        if k == order[0]:
            pl.semaphore_wait(barrier, greeted)
        copy = exchange(0, k, b_send, b_recv)
        copy.start()
        phases[0].append(copy)
    x_copies = []
    for k in range(1, replicas):
        other = (rep + k) % replicas
        copy = pltpu.make_async_remote_copy(
            src_ref=saved_hbm.at[:, pl.ds(pl.multiple_of(other * share, share), share)],
            dst_ref=x_all.at[pl.ds(pl.multiple_of(rep * rows, rows), rows)],
            send_sem=x_send.at[k], recv_sem=x_recv.at[k],
            device_id={"replica": other}, device_id_type=MESH,
        )
        copy.start()
        x_copies.append(copy)
    block(b_recv, me)[...] = pack(b_row, scaled, me)

    f_row, f_column = route_slots(f_routes[...], experts, cap)
    f_scale = to_column(f_gates[...])
    loads[1].wait()
    for k in order:
        block(f_send, flipped(me, k))[...] = pack(f_row, tokens[...], flipped(me, k))
        copy = exchange(1, k, f_send, f_recv)
        copy.start()
        phases[1].append(copy)
    block(f_recv, me)[...] = pack(f_row, tokens[...], me)

    loads[2].wait()
    loads[3].wait()
    loads[4].wait()
    pre[...] = jnp.dot(saved[...], w_gu[...], preferred_element_type=F32)
    loads[5].wait()

    for copy in phases[0]:
        copy.wait_recv()
    hidden_grad = jnp.dot(b_recv[...], w_down[...], preferred_element_type=F32)
    gate_pre, up_pre = pre[:, :hidden_units], pre[:, hidden_units:]
    sigma = jax.nn.sigmoid(gate_pre)
    mine = pl.ds(pl.multiple_of(rep * rows, rows), rows)
    g_all[mine, hidden_units:] = (hidden_grad * gate_pre * sigma).astype(BF16)
    g_all[mine, :hidden_units] = (
        hidden_grad * up_pre * sigma * (1.0 + gate_pre * (1.0 - sigma))
    ).astype(BF16)

    def pass_on(source, side):
        where = pl.ds(pl.multiple_of(source * rows, rows), rows)
        other = rep + (1 if side == 0 else -1)
        return pltpu.make_async_remote_copy(
            src_ref=g_all.at[where], dst_ref=g_all.at[where],
            send_sem=g_send.at[side, source], recv_sem=g_recv.at[source],
            device_id={"replica": other}, device_id_type=MESH,
        )

    @pl.when(rep < replicas - 1)
    def _():
        pass_on(rep, 0).start()

    @pl.when(rep > 0)
    def _():
        pass_on(rep, 1).start()

    for c in range(0, width, chunk):
        r_send[:, c:c + chunk] = transposed_dot(g_all[mine, :], w_gu[c:c + chunk, :]).astype(BF16)
    for k in order:
        copy = exchange(2, k, r_send, r_recv)
        copy.start()
        phases[2].append(copy)
    block(r_recv, me)[...] = block(r_send, me)[...]

    for copy in phases[1]:
        copy.wait_recv()
    pre[...] = jnp.dot(f_recv[...], w_gu[...], preferred_element_type=F32)
    gate_pre, up_pre = pre[:, :hidden_units], pre[:, hidden_units:]
    hidden = (gate_pre * jax.nn.sigmoid(gate_pre) * up_pre).astype(BF16)
    for c in range(0, width, chunk):
        o_send[:, c:c + chunk] = transposed_dot(hidden, w_down[c:c + chunk, :]).astype(BF16)
    for k in order:
        copy = exchange(3, k, o_send, o_recv)
        copy.start()
        phases[3].append(copy)
    block(o_recv, me)[...] = block(o_send, me)[...]

    def relay(step):
        low, high = rep - step, rep + step

        @pl.when(low >= 0)
        def _():
            pass_on(low, 0).wait_recv()

            @pl.when(rep < replicas - 1)
            def _():
                pass_on(low, 0).start()

        @pl.when(high < replicas)
        def _():
            pass_on(high, 1).wait_recv()

            @pl.when(rep > 0)
            def _():
                pass_on(high, 1).start()

    relay(1)

    for copy in phases[2]:
        copy.wait_recv()
    back = jnp.dot(spread_table(b_column, rows), r_recv[...], preferred_element_type=F32)
    local_v[...] = (cot[...].astype(F32) + back).astype(BF16)
    onward = pltpu.make_async_remote_copy(
        src_ref=local_v, dst_ref=received_hbm, send_sem=s_send, recv_sem=s_recv,
        device_id={"section": (section + sections - 1) % sections}, device_id_type=MESH,
    )
    onward.start()

    for step in range(2, replicas):
        relay(step)
    for copy in x_copies:
        copy.wait_recv()
    loads[6].wait()
    grads_v[...] = lax.dot_general(
        x_all[...], g_all[...], (((0,), (0,)), ((), ())), preferred_element_type=F32
    ).astype(BF16)
    store_grads = pltpu.make_async_copy(grads_v, grads_hbm, out_sem.at[0])
    store_grads.start()

    for copy in phases[3]:
        copy.wait_recv()
    back = jnp.dot(spread_table(f_column, rows), o_recv[...], preferred_element_type=F32)
    out_v[...] = (tokens[...].astype(F32) + f_scale * back).astype(BF16)
    store_out = pltpu.make_async_copy(out_v, out_hbm, out_sem.at[1])
    store_out.start()

    for phase in phases:
        for copy in phase:
            copy.wait_send()
    for copy in x_copies:
        copy.wait_send()
    for source in range(replicas):
        @pl.when((rep >= source) & (rep < replicas - 1))
        def _():
            pass_on(source, 0).wait_send()

        @pl.when((rep <= source) & (rep > 0))
        def _():
            pass_on(source, 1).wait_send()
    onward.wait()
    store_grads.wait()
    store_out.wait()


def solution(mesh):
    sections, experts, replicas = mesh.shape["section"], mesh.shape["expert"], mesh.shape["replica"]

    def shards(
        forward_tokens, forward_routes, forward_gates, backward_cotangent, backward_routes, backward_gates,
        saved_rows, gate_weight, up_weight, down_weight,
    ):
        count, width = forward_tokens.shape[1:]
        hidden_units = gate_weight.shape[3]
        slots = saved_rows.shape[2] // experts
        cap = -(-slots // 16) * 16
        saved = saved_rows[0, 0]
        if cap != slots:
            saved = jnp.pad(saved.reshape(experts, slots, width), ((0, 0), (0, cap - slots), (0, 0)))
            saved = saved.reshape(experts * cap, width)
        rows = experts * cap
        share = width // replicas
        buffer = pltpu.VMEM((rows, width), BF16)
        dma = pltpu.SemaphoreType.DMA
        whole = pl.BlockSpec(memory_space=pltpu.VMEM)
        anywhere = pl.BlockSpec(memory_space=pl.ANY)
        out, received, grads = pl.pallas_call(
            functools.partial(kernel, sections, experts, replicas, cap),
            out_shape=[
                jax.ShapeDtypeStruct((count, width), BF16),
                jax.ShapeDtypeStruct((count, width), BF16),
                jax.ShapeDtypeStruct((share, 2 * hidden_units), BF16),
            ],
            in_specs=[whole] * 4 + [anywhere] * 6,
            out_specs=[anywhere] * 3,
            scratch_shapes=[
                pltpu.VMEM((count, width), BF16),
                pltpu.VMEM((count, width), BF16),
                buffer,
                pltpu.VMEM((width, 2 * hidden_units), BF16),
                pltpu.VMEM((width, hidden_units), BF16),
                buffer, buffer, buffer, buffer,
                buffer, buffer, buffer, buffer,
                pltpu.VMEM((replicas * rows, share), BF16),
                pltpu.VMEM((replicas * rows, 2 * hidden_units), BF16),
                pltpu.VMEM((rows, 2 * hidden_units), F32),
                pltpu.VMEM((count, width), BF16),
                pltpu.VMEM((count, width), BF16),
                pltpu.VMEM((share, 2 * hidden_units), BF16),
                dma((7,)),
                dma((4, experts)),
                dma((4, experts)),
                dma((replicas,)),
                dma((replicas,)),
                dma((2, replicas)),
                dma((replicas,)),
                dma,
                dma,
                dma((2,)),
            ],
            compiler_params=pltpu.CompilerParams(
                collective_id=0, has_side_effects=True, vmem_limit_bytes=48 * 1024 * 1024
            ),
        )(
            forward_routes.reshape(1, count), forward_gates.reshape(1, count),
            backward_routes.reshape(1, count), backward_gates.reshape(1, count),
            forward_tokens[0], backward_cotangent[0], saved,
            gate_weight[0, 0], up_weight[0, 0], down_weight[0, 0],
        )
        return out[None], received[None], grads[None, None]

    tokens = P("section", ("expert", "replica"), None)
    weights = P("section", "expert", None, None)
    rows = P("section", "expert", "replica", None)
    return jax.shard_map(
        shards, mesh=mesh, in_specs=(tokens,) * 6 + (rows,) + (weights,) * 3,
        out_specs=(tokens, tokens, rows), check_vma=False,
    )
```

```python
import functools

import jax
import jax.numpy as jnp
from jax import lax
from jax.experimental import pallas as pl
from jax.experimental.pallas import tpu as pltpu
from jax.sharding import PartitionSpec as P

MESH = pl.DeviceIdType.MESH
BF16, F32 = jnp.bfloat16, jnp.float32
PARTS = 2


def flipped(index, mask):
    for bit in range(mask.bit_length()):
        if (mask >> bit) & 1:
            index = index + (1 << bit) * (1 - 2 * ((index // (1 << bit)) % 2))
    return index


def route_slots(routes, experts, cap):
    tokens = routes.shape[1]
    height = -(-experts // 16) * 16
    member = (lax.broadcasted_iota(jnp.int32, (height, tokens), 0) == routes).astype(F32)
    above = lax.broadcasted_iota(jnp.int32, (tokens, tokens), 0)
    across = lax.broadcasted_iota(jnp.int32, (tokens, tokens), 1)
    before = (above < across).astype(F32).astype(BF16)
    earlier = jnp.dot(member.astype(BF16), before, preferred_element_type=F32)
    slot = jnp.sum(earlier * member, axis=0, keepdims=True)
    row = routes.astype(F32) * cap + slot
    return row, to_column(row)


def to_column(row):
    tokens = row.shape[1]
    above = lax.broadcasted_iota(jnp.int32, (tokens, tokens), 0)
    across = lax.broadcasted_iota(jnp.int32, (tokens, tokens), 1)
    return jnp.sum(jnp.where(above == across, row, 0.0), axis=1, keepdims=True)


def spread_table(column, rows):
    across = lax.broadcasted_iota(jnp.int32, (column.shape[0], rows), 1).astype(F32)
    return (across == column).astype(F32).astype(BF16)


def transposed_dot(a, b):
    return lax.dot_general(a, b, (((1,), (1,)), ((), ())), preferred_element_type=F32)


def kernel(
    sections, experts, replicas, cap,
    f_routes, f_gates, b_routes, b_gates, tokens_hbm, cot_hbm, saved_hbm, gate_hbm, up_hbm, down_hbm,
    out_hbm, received_hbm, grads_hbm,
    tokens, cot, saved, w_gu, w_down, f_send, f_recv, b_send, b_recv,
    o_send, o_recv, r_send, r_recv, x_all, g_all, pre, out_v, local_v, grads_v, total,
    local_sem, a2a_send, a2a_recv, x_send, x_recv, g_send, g_recv, s_send, s_recv, out_sem,
):
    section, me, rep = lax.axis_index("section"), lax.axis_index("expert"), lax.axis_index("replica")
    count, width = tokens.shape
    rows = experts * cap
    hidden_units = w_down.shape[1]
    share = width // replicas
    chunk = min(512, width)

    barrier = pltpu.get_barrier_semaphore()
    greeted = 0
    for k in range(1, experts):
        pl.semaphore_signal(barrier, inc=1, device_id={"expert": flipped(me, k)}, device_id_type=MESH)
        greeted += 1
    for k in range(1, replicas):
        pl.semaphore_signal(barrier, inc=1, device_id={"replica": (rep + k) % replicas}, device_id_type=MESH)
        greeted += 1
    for k in sorted({1, sections - 1}):
        pl.semaphore_signal(barrier, inc=1, device_id={"section": (section + k) % sections}, device_id_type=MESH)
        greeted += 1

    loads = [
        pltpu.make_async_copy(src, dst, local_sem.at[i])
        for i, (src, dst) in enumerate([
            (cot_hbm, cot),
            (tokens_hbm, tokens),
            (saved_hbm, saved),
            (gate_hbm, w_gu.at[:, pl.ds(0, hidden_units)]),
            (up_hbm, w_gu.at[:, pl.ds(hidden_units, hidden_units)]),
            (down_hbm, w_down),
            (saved_hbm.at[:, pl.ds(pl.multiple_of(rep * share, share), share)],
             x_all.at[pl.ds(pl.multiple_of(rep * rows, rows), rows)]),
        ])
    ]
    for load in loads:
        load.start()

    def block(ref, index):
        return ref.at[pl.ds(pl.multiple_of(index * cap, cap), cap)]

    def exchange(phase, k, src, dst):
        other = flipped(me, k)
        return pltpu.make_async_remote_copy(
            src_ref=block(src, other), dst_ref=block(dst, me),
            send_sem=a2a_send.at[phase, k], recv_sem=a2a_recv.at[phase, k],
            device_id={"expert": other}, device_id_type=MESH,
        )

    order = list(range(experts - 1, 0, -1))

    def pack(row, values, index):
        down = lax.broadcasted_iota(jnp.int32, (cap, count), 0).astype(F32) + (index * cap).astype(F32)
        table = (down == row).astype(F32).astype(BF16)
        return jnp.dot(table, values, preferred_element_type=F32).astype(BF16)

    b_row, b_column = route_slots(b_routes[...], experts, cap)
    b_scale = to_column(b_gates[...])
    loads[0].wait()
    scaled = (b_scale * cot[...].astype(F32)).astype(BF16)
    phases = [
        [exchange(phase, k, src, dst) for k in order]
        for phase, (src, dst) in enumerate(
            [(b_send, b_recv), (f_send, f_recv), (r_send, r_recv), (o_send, o_recv)]
        )
    ]
    x_copies = [
        pltpu.make_async_remote_copy(
            src_ref=saved_hbm.at[:, pl.ds(pl.multiple_of((rep + k) % replicas * share, share), share)],
            dst_ref=x_all.at[pl.ds(pl.multiple_of(rep * rows, rows), rows)],
            send_sem=x_send.at[k], recv_sem=x_recv.at[k],
            device_id={"replica": (rep + k) % replicas}, device_id_type=MESH,
        )
        for k in range(1, replicas)
    ]
    for k, copy in zip(order, phases[0]):
        block(b_send, flipped(me, k))[...] = pack(b_row, scaled, flipped(me, k))
        if k == order[0]:
            pl.semaphore_wait(barrier, greeted)
        copy.start()
    for copy in x_copies:
        copy.start()
    block(b_recv, me)[...] = pack(b_row, scaled, me)

    f_row, f_column = route_slots(f_routes[...], experts, cap)
    f_scale = to_column(f_gates[...])
    loads[1].wait()
    for k in order:
        block(f_send, flipped(me, k))[...] = pack(f_row, tokens[...], flipped(me, k))
    block(f_recv, me)[...] = pack(f_row, tokens[...], me)

    loads[2].wait()
    loads[3].wait()
    loads[4].wait()
    pre[...] = jnp.dot(saved[...], w_gu[...], preferred_element_type=F32)
    loads[5].wait()
    loads[6].wait()

    def follow(phase):
        for copy in phases[phase - 1]:
            copy.wait_send()
        for copy in phases[phase]:
            copy.start()

    follow(1)

    for copy in phases[0]:
        copy.wait_recv()
    hidden_grad = jnp.dot(b_recv[...], w_down[...], preferred_element_type=F32)
    gate_pre, up_pre = pre[:, :hidden_units], pre[:, hidden_units:]
    sigma = jax.nn.sigmoid(gate_pre)
    mine = pl.ds(pl.multiple_of(rep * rows, rows), rows)
    g_all[mine, hidden_units:] = (hidden_grad * gate_pre * sigma).astype(BF16)
    g_all[mine, :hidden_units] = (
        hidden_grad * up_pre * sigma * (1.0 + gate_pre * (1.0 - sigma))
    ).astype(BF16)
    part = rows // PARTS

    def pass_on(source, side, piece):
        where = pl.ds(pl.multiple_of(source * rows + piece * part, part), part)
        return pltpu.make_async_remote_copy(
            src_ref=g_all.at[where], dst_ref=g_all.at[where],
            send_sem=g_send.at[side, source, piece], recv_sem=g_recv.at[source, piece],
            device_id={"replica": rep + (1 if side == 0 else -1)}, device_id_type=MESH,
        )

    for piece in range(PARTS):
        @pl.when(rep < replicas - 1)
        def _():
            pass_on(rep, 0, piece).start()

        @pl.when(rep > 0)
        def _():
            pass_on(rep, 1, piece).start()

    def relay(step, piece):
        low, high = rep - step, rep + step

        @pl.when(low >= 0)
        def _():
            pass_on(low, 0, piece).wait_recv()

            @pl.when(rep < replicas - 1)
            def _():
                pass_on(low, 0, piece).start()

        @pl.when(high < replicas)
        def _():
            pass_on(high, 1, piece).wait_recv()

            @pl.when(rep > 0)
            def _():
                pass_on(high, 1, piece).start()

    def term(source):
        where = pl.ds(pl.multiple_of(source * rows, rows), rows)
        return lax.dot_general(
            x_all[where, :], g_all[where, :], (((0,), (0,)), ((), ())), preferred_element_type=F32
        )

    def add_terms(step):
        low, high = rep - step, rep + step

        @pl.when(low >= 0)
        def _():
            x_copies[step - 1].wait_recv()
            total[...] += term(low)

        @pl.when(high < replicas)
        def _():
            x_copies[replicas - step - 1].wait_recv()
            total[...] += term(high)

    for c in range(0, width, chunk):
        r_send[:, c:c + chunk] = transposed_dot(g_all[mine, :], w_gu[c:c + chunk, :]).astype(BF16)
    block(r_recv, me)[...] = block(r_send, me)[...]
    total[...] = term(rep)

    follow(2)
    for copy in phases[1]:
        copy.wait_recv()
    pre[...] = jnp.dot(f_recv[...], w_gu[...], preferred_element_type=F32)
    gate_pre, up_pre = pre[:, :hidden_units], pre[:, hidden_units:]
    hidden = (gate_pre * jax.nn.sigmoid(gate_pre) * up_pre).astype(BF16)
    for c in range(0, width, chunk):
        o_send[:, c:c + chunk] = transposed_dot(hidden, w_down[c:c + chunk, :]).astype(BF16)
    block(o_recv, me)[...] = block(o_send, me)[...]

    for piece in range(PARTS):
        relay(1, piece)
    follow(3)
    add_terms(1)

    for copy in phases[2]:
        copy.wait_recv()
    back = jnp.dot(spread_table(b_column, rows), r_recv[...], preferred_element_type=F32)
    local_v[...] = (cot[...].astype(F32) + back).astype(BF16)
    onward = pltpu.make_async_remote_copy(
        src_ref=local_v, dst_ref=received_hbm, send_sem=s_send, recv_sem=s_recv,
        device_id={"section": (section + sections - 1) % sections}, device_id_type=MESH,
    )
    onward.start()

    for step in range(2, replicas):
        for piece in range(PARTS):
            relay(step, piece)
        add_terms(step)
    grads_v[...] = total[...].astype(BF16)
    store_grads = pltpu.make_async_copy(grads_v, grads_hbm, out_sem.at[0])
    store_grads.start()

    for copy in phases[3]:
        copy.wait_recv()
    back = jnp.dot(spread_table(f_column, rows), o_recv[...], preferred_element_type=F32)
    out_v[...] = (tokens[...].astype(F32) + f_scale * back).astype(BF16)
    store_out = pltpu.make_async_copy(out_v, out_hbm, out_sem.at[1])
    store_out.start()

    for copy in phases[3] + x_copies:
        copy.wait_send()
    for source in range(replicas):
        @pl.when((rep >= source) & (rep < replicas - 1))
        def _():
            for piece in range(PARTS):
                pass_on(source, 0, piece).wait_send()

        @pl.when((rep <= source) & (rep > 0))
        def _():
            for piece in range(PARTS):
                pass_on(source, 1, piece).wait_send()
    onward.wait()
    store_grads.wait()
    store_out.wait()


def solution(mesh):
    sections, experts, replicas = mesh.shape["section"], mesh.shape["expert"], mesh.shape["replica"]

    def shards(
        forward_tokens, forward_routes, forward_gates, backward_cotangent, backward_routes, backward_gates,
        saved_rows, gate_weight, up_weight, down_weight,
    ):
        count, width = forward_tokens.shape[1:]
        hidden_units = gate_weight.shape[3]
        slots = saved_rows.shape[2] // experts
        cap = -(-slots // 16) * 16
        saved = saved_rows[0, 0]
        if cap != slots:
            saved = jnp.pad(saved.reshape(experts, slots, width), ((0, 0), (0, cap - slots), (0, 0)))
            saved = saved.reshape(experts * cap, width)
        rows = experts * cap
        share = width // replicas
        buffer = pltpu.VMEM((rows, width), BF16)
        dma = pltpu.SemaphoreType.DMA
        whole = pl.BlockSpec(memory_space=pltpu.VMEM)
        anywhere = pl.BlockSpec(memory_space=pl.ANY)
        out, received, grads = pl.pallas_call(
            functools.partial(kernel, sections, experts, replicas, cap),
            out_shape=[
                jax.ShapeDtypeStruct((count, width), BF16),
                jax.ShapeDtypeStruct((count, width), BF16),
                jax.ShapeDtypeStruct((share, 2 * hidden_units), BF16),
            ],
            in_specs=[whole] * 4 + [anywhere] * 6,
            out_specs=[anywhere] * 3,
            scratch_shapes=[
                pltpu.VMEM((count, width), BF16),
                pltpu.VMEM((count, width), BF16),
                buffer,
                pltpu.VMEM((width, 2 * hidden_units), BF16),
                pltpu.VMEM((width, hidden_units), BF16),
                buffer, buffer, buffer, buffer,
                buffer, buffer, buffer, buffer,
                pltpu.VMEM((replicas * rows, share), BF16),
                pltpu.VMEM((replicas * rows, 2 * hidden_units), BF16),
                pltpu.VMEM((rows, 2 * hidden_units), F32),
                pltpu.VMEM((count, width), BF16),
                pltpu.VMEM((count, width), BF16),
                pltpu.VMEM((share, 2 * hidden_units), BF16),
                pltpu.VMEM((share, 2 * hidden_units), F32),
                dma((7,)),
                dma((4, experts)),
                dma((4, experts)),
                dma((replicas,)),
                dma((replicas,)),
                dma((2, replicas, PARTS)),
                dma((replicas, PARTS)),
                dma,
                dma,
                dma((2,)),
            ],
            compiler_params=pltpu.CompilerParams(
                collective_id=0, has_side_effects=True, vmem_limit_bytes=62 * 1024 * 1024
            ),
        )(
            forward_routes.reshape(1, count), forward_gates.reshape(1, count),
            backward_routes.reshape(1, count), backward_gates.reshape(1, count),
            forward_tokens[0], backward_cotangent[0], saved,
            gate_weight[0, 0], up_weight[0, 0], down_weight[0, 0],
        )
        return out[None], received[None], grads[None, None]

    tokens = P("section", ("expert", "replica"), None)
    weights = P("section", "expert", None, None)
    rows = P("section", "expert", "replica", None)
    return jax.shard_map(
        shards, mesh=mesh, in_specs=(tokens,) * 6 + (rows,) + (weights,) * 3,
        out_specs=(tokens, tokens, rows), check_vma=False,
    )
```

```python
import functools

import jax
import jax.numpy as jnp
from jax import lax
from jax.experimental import pallas as pl
from jax.experimental.pallas import tpu as pltpu
from jax.sharding import PartitionSpec as P

MESH = pl.DeviceIdType.MESH
BF16, F32 = jnp.bfloat16, jnp.float32
PARTS = 2


def flipped(index, mask):
    for bit in range(mask.bit_length()):
        if (mask >> bit) & 1:
            index = index + (1 << bit) * (1 - 2 * ((index // (1 << bit)) % 2))
    return index


def route_slots(routes, experts, cap):
    tokens = routes.shape[1]
    height = -(-experts // 16) * 16
    member = (lax.broadcasted_iota(jnp.int32, (height, tokens), 0) == routes).astype(F32)
    above = lax.broadcasted_iota(jnp.int32, (tokens, tokens), 0)
    across = lax.broadcasted_iota(jnp.int32, (tokens, tokens), 1)
    before = (above < across).astype(F32).astype(BF16)
    earlier = jnp.dot(member.astype(BF16), before, preferred_element_type=F32)
    slot = jnp.sum(earlier * member, axis=0, keepdims=True)
    row = routes.astype(F32) * cap + slot
    return row, to_column(row)


def to_column(row):
    tokens = row.shape[1]
    above = lax.broadcasted_iota(jnp.int32, (tokens, tokens), 0)
    across = lax.broadcasted_iota(jnp.int32, (tokens, tokens), 1)
    return jnp.sum(jnp.where(above == across, row, 0.0), axis=1, keepdims=True)


def spread_table(column, rows):
    across = lax.broadcasted_iota(jnp.int32, (column.shape[0], rows), 1).astype(F32)
    return (across == column).astype(F32).astype(BF16)


def transposed_dot(a, b):
    return lax.dot_general(a, b, (((1,), (1,)), ((), ())), preferred_element_type=F32)


def kernel(
    sections, experts, replicas, cap,
    f_routes_hbm, f_gates_hbm, b_routes_hbm, b_gates_hbm, tokens_hbm, cot_hbm, saved_hbm, gate_hbm, up_hbm, down_hbm,
    out_v, received, grads_v,
    f_routes, f_gates, b_routes, b_gates, tokens, cot, saved, w_gu, w_down, f_send, f_recv, b_send, b_recv,
    o_send, o_recv, r_send, r_recv, x_all, g_all, pre, local_v, total,
    local_sem, a2a_send, a2a_recv, x_send, x_recv, g_send, g_recv, s_send, s_recv,
):
    section, me, rep = lax.axis_index("section"), lax.axis_index("expert"), lax.axis_index("replica")
    count, width = tokens.shape
    rows = experts * cap
    hidden_units = w_down.shape[1]
    share = width // replicas
    chunk = min(512, width)

    barrier = pltpu.get_barrier_semaphore()
    greeted = 0
    for k in range(1, experts):
        pl.semaphore_signal(barrier, inc=1, device_id={"expert": flipped(me, k)}, device_id_type=MESH)
        greeted += 1
    for k in range(1, replicas):
        pl.semaphore_signal(barrier, inc=1, device_id={"replica": (rep + k) % replicas}, device_id_type=MESH)
        greeted += 1
    for k in sorted({1, sections - 1}):
        pl.semaphore_signal(barrier, inc=1, device_id={"section": (section + k) % sections}, device_id_type=MESH)
        greeted += 1

    loads = [
        pltpu.make_async_copy(src, dst, local_sem.at[i])
        for i, (src, dst) in enumerate([
            (cot_hbm, cot),
            (tokens_hbm, tokens),
            (saved_hbm, saved),
            (gate_hbm, w_gu.at[:, pl.ds(0, hidden_units)]),
            (up_hbm, w_gu.at[:, pl.ds(hidden_units, hidden_units)]),
            (down_hbm, w_down),
            (saved_hbm.at[:, pl.ds(pl.multiple_of(rep * share, share), share)],
             x_all.at[pl.ds(pl.multiple_of(rep * rows, rows), rows)]),
            (b_routes_hbm, b_routes),
            (b_gates_hbm, b_gates),
            (f_routes_hbm, f_routes),
            (f_gates_hbm, f_gates),
        ])
    ]
    for load in loads[7:] + loads[:7]:
        load.start()

    def block(ref, index):
        return ref.at[pl.ds(pl.multiple_of(index * cap, cap), cap)]

    def exchange(phase, k, src, dst):
        other = flipped(me, k)
        return pltpu.make_async_remote_copy(
            src_ref=block(src, other), dst_ref=block(dst, me),
            send_sem=a2a_send.at[phase, k], recv_sem=a2a_recv.at[phase, k],
            device_id={"expert": other}, device_id_type=MESH,
        )

    order = list(range(experts - 1, 0, -1))

    def pack(row, values, index):
        down = lax.broadcasted_iota(jnp.int32, (cap, count), 0).astype(F32) + (index * cap).astype(F32)
        table = (down == row).astype(F32).astype(BF16)
        return jnp.dot(table, values, preferred_element_type=F32).astype(BF16)

    loads[7].wait()
    loads[8].wait()
    b_row, b_column = route_slots(b_routes[...], experts, cap)
    b_scale = to_column(b_gates[...])
    loads[0].wait()
    scaled = (b_scale * cot[...].astype(F32)).astype(BF16)
    phases = [
        [exchange(phase, k, src, dst) for k in order]
        for phase, (src, dst) in enumerate(
            [(b_send, b_recv), (f_send, f_recv), (r_send, r_recv), (o_send, o_recv)]
        )
    ]
    x_copies = [
        pltpu.make_async_remote_copy(
            src_ref=saved_hbm.at[:, pl.ds(pl.multiple_of((rep + k) % replicas * share, share), share)],
            dst_ref=x_all.at[pl.ds(pl.multiple_of(rep * rows, rows), rows)],
            send_sem=x_send.at[k], recv_sem=x_recv.at[k],
            device_id={"replica": (rep + k) % replicas}, device_id_type=MESH,
        )
        for k in range(1, replicas)
    ]
    for k, copy in zip(order, phases[0]):
        block(b_send, flipped(me, k))[...] = pack(b_row, scaled, flipped(me, k))
        if k == order[0]:
            pl.semaphore_wait(barrier, greeted)
            for x_copy in x_copies:
                x_copy.start()
        copy.start()
    block(b_recv, me)[...] = pack(b_row, scaled, me)

    loads[9].wait()
    loads[10].wait()
    f_row, f_column = route_slots(f_routes[...], experts, cap)
    f_scale = to_column(f_gates[...])
    loads[1].wait()
    for k in order:
        block(f_send, flipped(me, k))[...] = pack(f_row, tokens[...], flipped(me, k))
    block(f_recv, me)[...] = pack(f_row, tokens[...], me)

    loads[2].wait()
    loads[3].wait()
    loads[4].wait()
    pre[...] = jnp.dot(saved[...], w_gu[...], preferred_element_type=F32)
    loads[5].wait()
    loads[6].wait()

    def follow(phase):
        for copy in phases[phase - 1]:
            copy.wait_send()
        for copy in phases[phase]:
            copy.start()

    follow(1)

    for copy in phases[0]:
        copy.wait_recv()
    hidden_grad = jnp.dot(b_recv[...], w_down[...], preferred_element_type=F32)
    gate_pre, up_pre = pre[:, :hidden_units], pre[:, hidden_units:]
    sigma = jax.nn.sigmoid(gate_pre)
    mine = pl.ds(pl.multiple_of(rep * rows, rows), rows)
    g_all[mine, hidden_units:] = (hidden_grad * gate_pre * sigma).astype(BF16)
    g_all[mine, :hidden_units] = (
        hidden_grad * up_pre * sigma * (1.0 + gate_pre * (1.0 - sigma))
    ).astype(BF16)
    part = rows // PARTS

    def pass_on(source, side, piece):
        where = pl.ds(pl.multiple_of(source * rows + piece * part, part), part)
        return pltpu.make_async_remote_copy(
            src_ref=g_all.at[where], dst_ref=g_all.at[where],
            send_sem=g_send.at[side, source, piece], recv_sem=g_recv.at[source, piece],
            device_id={"replica": rep + (1 if side == 0 else -1)}, device_id_type=MESH,
        )

    for piece in range(PARTS):
        @pl.when(rep < replicas - 1)
        def _():
            pass_on(rep, 0, piece).start()

        @pl.when(rep > 0)
        def _():
            pass_on(rep, 1, piece).start()

    def relay(step, piece):
        low, high = rep - step, rep + step

        @pl.when(low >= 0)
        def _():
            pass_on(low, 0, piece).wait_recv()

            @pl.when(rep < replicas - 1)
            def _():
                pass_on(low, 0, piece).start()

        @pl.when(high < replicas)
        def _():
            pass_on(high, 1, piece).wait_recv()

            @pl.when(rep > 0)
            def _():
                pass_on(high, 1, piece).start()

    def term(source):
        where = pl.ds(pl.multiple_of(source * rows, rows), rows)
        return lax.dot_general(
            x_all[where, :], g_all[where, :], (((0,), (0,)), ((), ())), preferred_element_type=F32
        )

    def add_terms(step):
        low, high = rep - step, rep + step

        @pl.when(low >= 0)
        def _():
            x_copies[step - 1].wait_recv()
            total[...] += term(low)

        @pl.when(high < replicas)
        def _():
            x_copies[replicas - step - 1].wait_recv()
            total[...] += term(high)

    for c in range(0, width, chunk):
        r_send[:, c:c + chunk] = transposed_dot(g_all[mine, :], w_gu[c:c + chunk, :]).astype(BF16)
    block(r_recv, me)[...] = block(r_send, me)[...]
    total[...] = term(rep)

    follow(2)
    for copy in phases[1]:
        copy.wait_recv()
    pre[...] = jnp.dot(f_recv[...], w_gu[...], preferred_element_type=F32)
    gate_pre, up_pre = pre[:, :hidden_units], pre[:, hidden_units:]
    hidden = (gate_pre * jax.nn.sigmoid(gate_pre) * up_pre).astype(BF16)
    for c in range(0, width, chunk):
        o_send[:, c:c + chunk] = transposed_dot(hidden, w_down[c:c + chunk, :]).astype(BF16)
    block(o_recv, me)[...] = block(o_send, me)[...]

    for piece in range(PARTS):
        relay(1, piece)
    follow(3)
    add_terms(1)

    for copy in phases[2]:
        copy.wait_recv()
    back = jnp.dot(spread_table(b_column, rows), r_recv[...], preferred_element_type=F32)
    local_v[...] = (cot[...].astype(F32) + back).astype(BF16)
    onward = pltpu.make_async_remote_copy(
        src_ref=local_v, dst_ref=received, send_sem=s_send, recv_sem=s_recv,
        device_id={"section": (section + sections - 1) % sections}, device_id_type=MESH,
    )
    onward.start()

    for step in range(2, replicas):
        for piece in range(PARTS):
            relay(step, piece)
        add_terms(step)
    grads_v[...] = total[...].astype(BF16)

    for copy in phases[3]:
        copy.wait_recv()
    back = jnp.dot(spread_table(f_column, rows), o_recv[...], preferred_element_type=F32)
    out_v[...] = (tokens[...].astype(F32) + f_scale * back).astype(BF16)

    for copy in phases[3] + x_copies:
        copy.wait_send()
    for source in range(replicas):
        @pl.when((rep >= source) & (rep < replicas - 1))
        def _():
            for piece in range(PARTS):
                pass_on(source, 0, piece).wait_send()

        @pl.when((rep <= source) & (rep > 0))
        def _():
            for piece in range(PARTS):
                pass_on(source, 1, piece).wait_send()
    onward.wait()


def store(out_v, received, grads_v, out_hbm, received_hbm, grads_hbm, sem):
    pairs = [(out_v, out_hbm), (received, received_hbm), (grads_v, grads_hbm)]
    copies = [pltpu.make_async_copy(src, dst, sem.at[i]) for i, (src, dst) in enumerate(pairs)]
    for copy in copies:
        copy.start()
    for copy in copies:
        copy.wait()


def solution(mesh):
    sections, experts, replicas = mesh.shape["section"], mesh.shape["expert"], mesh.shape["replica"]

    def shards(
        forward_tokens, forward_routes, forward_gates, backward_cotangent, backward_routes, backward_gates,
        saved_rows, gate_weight, up_weight, down_weight,
    ):
        count, width = forward_tokens.shape[1:]
        hidden_units = gate_weight.shape[3]
        slots = saved_rows.shape[2] // experts
        cap = -(-slots // 16) * 16
        saved = saved_rows[0, 0]
        if cap != slots:
            saved = jnp.pad(saved.reshape(experts, slots, width), ((0, 0), (0, cap - slots), (0, 0)))
            saved = saved.reshape(experts * cap, width)
        rows = experts * cap
        share = width // replicas
        buffer = pltpu.VMEM((rows, width), BF16)
        dma = pltpu.SemaphoreType.DMA
        whole = pl.BlockSpec(memory_space=pltpu.VMEM)
        far = pl.BlockSpec(memory_space=pltpu.HBM)
        held = pl.pallas_call(
            functools.partial(kernel, sections, experts, replicas, cap),
            out_shape=[
                pltpu.VMEM((count, width), BF16),
                pltpu.VMEM((count, width), BF16),
                pltpu.VMEM((share, 2 * hidden_units), BF16),
            ],
            in_specs=[far] * 10,
            out_specs=[whole] * 3,
            scratch_shapes=[
                pltpu.VMEM((1, count), jnp.int32),
                pltpu.VMEM((1, count), F32),
                pltpu.VMEM((1, count), jnp.int32),
                pltpu.VMEM((1, count), F32),
                pltpu.VMEM((count, width), BF16),
                pltpu.VMEM((count, width), BF16),
                buffer,
                pltpu.VMEM((width, 2 * hidden_units), BF16),
                pltpu.VMEM((width, hidden_units), BF16),
                buffer, buffer, buffer, buffer,
                buffer, buffer, buffer, buffer,
                pltpu.VMEM((replicas * rows, share), BF16),
                pltpu.VMEM((replicas * rows, 2 * hidden_units), BF16),
                pltpu.VMEM((rows, 2 * hidden_units), F32),
                pltpu.VMEM((count, width), BF16),
                pltpu.VMEM((share, 2 * hidden_units), F32),
                dma((11,)),
                dma((4, experts)),
                dma((4, experts)),
                dma((replicas,)),
                dma((replicas,)),
                dma((2, replicas, PARTS)),
                dma((replicas, PARTS)),
                dma,
                dma,
            ],
            compiler_params=pltpu.CompilerParams(
                collective_id=0, has_side_effects=True, vmem_limit_bytes=44 * 1024 * 1024
            ),
        )(
            *(
                pltpu.with_memory_space_constraint(value, pltpu.HBM)
                for value in (
                    forward_routes.reshape(1, count), forward_gates.reshape(1, count),
                    backward_routes.reshape(1, count), backward_gates.reshape(1, count),
                    forward_tokens[0], backward_cotangent[0], saved,
                    gate_weight[0, 0], up_weight[0, 0], down_weight[0, 0],
                )
            ),
        )
        out, received, grads = pl.pallas_call(
            store,
            out_shape=[jax.ShapeDtypeStruct(value.shape, value.dtype) for value in held],
            in_specs=[whole] * 3,
            out_specs=[far] * 3,
            scratch_shapes=[dma((3,))],
        )(*(pltpu.with_memory_space_constraint(value, pltpu.VMEM) for value in held))
        return out[None], received[None], grads[None, None]

    tokens = P("section", ("expert", "replica"), None)
    weights = P("section", "expert", None, None)
    rows = P("section", "expert", "replica", None)
    return jax.shard_map(
        shards, mesh=mesh, in_specs=(tokens,) * 6 + (rows,) + (weights,) * 3,
        out_specs=(tokens, tokens, rows), check_vma=False,
    )
```
